32 devices in a mesh: clip: 2 (over y), tm: 4 (over z), row: 2 (over x), col: 2 (over core).
Axes of the slice: x: 2, y: 2, z: 4, core: 2. Of those that a mesh axis runs over, the one named last changes fastest.
Arguments:
- right_side: float32 [3, 16, 64, 1024], P(None, ('clip', 'tm'), 'row', 'col'), parts along dimension 1, may hold values from -8 to 8
- screening: float32 [16, 64, 1024], P(('clip', 'tm'), 'row', 'col'), parts along dimension 0, may hold values from 0.05 to 0.5
- time_weight: float32 [16, 64, 1024], P(('clip', 'tm'), 'row', 'col'), parts along dimension 0, may hold values from 0.2 to 5
- row_weight: float32 [16, 64, 1024], P(('clip', 'tm'), 'row', 'col'), parts along dimension 0, may hold values from 0.2 to 5
- column_weight: float32 [16, 64, 1024], P(('clip', 'tm'), 'row', 'col'), parts along dimension 0, may hold values from 0.2 to 5
Outputs:
- solution_field: float32 [3, 16, 64, 1024], P(None, ('clip', 'tm'), 'row', 'col'), parts along dimension 1
- residual: float32 [3, 16, 64, 1024], P(None, ('clip', 'tm'), 'row', 'col'), parts along dimension 1
The draws below stay inside these ranges and needn't reach their ends.
There are 2 independent parts, one for each index of `clip`. The reference program is written for one: setup_inputs(seed, part) draws one part's arguments, and reference() takes and returns one part's arrays. A program takes and returns all parts, laid end to end along the dimension named above; each array names one. Nothing has to cross between parts.
All inputs are finite; a program needn't handle non-finite values.
Results may differ from the reference program's by a relative error of at most 0.0001.
Values sent between devices are 32-bit elements; how exact they have to be, the bound alone decides.
A program may use at most 64 MiB of HBM per device.

```python
import math
import jax
import jax.numpy as jnp

CH = 3
ITERS = 2
NF = 8
NY = 64
NX = 1024


def steps_of(key, shape, pieces, smallest, high):
    level, own = 1.0, jax.random.fold_in(key, 6)
    for axis_at, shards_of in pieces:
        draws = jnp.exp(jax.random.uniform(jax.random.fold_in(own, axis_at), (shards_of,), jnp.float32, smallest / len(pieces), high / len(pieces)))
        level = level * jnp.repeat(draws, shape[axis_at] // shards_of).reshape([-1 if axis == axis_at else 1 for axis in range(len(shape))])
    return level


def scatter_about(rng, dims, scale, reach, pieces=(), held_as=jnp.bfloat16):
    result = jax.random.normal(rng, dims, jnp.float32) * scale
    if len(pieces) > 0:
        result = steps_of(rng, dims, pieces, -0.22, 0.18) * result
    return jnp.clip(result, min=-reach, max=reach).astype(held_as)


def setup_inputs(seed: int = 0, part: int = 0) -> dict:
    keys = jax.random.split(jax.random.key(seed), 6)
    own_keys = jax.random.split(jax.random.fold_in(keys[5], part), 6)
    return {
        "right_side": scatter_about(own_keys[0], (CH, NF, NY, NX), 1.0, 8.0, ((1, 4), (2, 2), (3, 2)), jnp.float32),
        "screening": jnp.clip(jnp.exp(math.log(0.5) - 2.3025851 * jax.random.uniform(own_keys[1], (NF, NY, NX), jnp.float32) ** steps_of(own_keys[1], (NF, NY, NX), ((0, 4), (1, 2), (2, 2)), -0.2, 0.2)), 0.05, 0.5),
        "time_weight": jnp.clip(jnp.exp(math.log(5.0) - 3.218876 * jax.random.uniform(own_keys[2], (NF, NY, NX), jnp.float32) ** steps_of(own_keys[2], (NF, NY, NX), ((0, 4), (1, 2), (2, 2)), -0.2, 0.2)), 0.2, 5.0),
        "row_weight": jnp.clip(jnp.exp(math.log(5.0) - 3.218876 * jax.random.uniform(own_keys[3], (NF, NY, NX), jnp.float32) ** steps_of(own_keys[3], (NF, NY, NX), ((0, 4), (1, 2), (2, 2)), -0.2, 0.2)), 0.2, 5.0),
        "column_weight": jnp.clip(jnp.exp(math.log(5.0) - 3.218876 * jax.random.uniform(own_keys[4], (NF, NY, NX), jnp.float32) ** steps_of(own_keys[4], (NF, NY, NX), ((0, 4), (1, 2), (2, 2)), -0.2, 0.2)), 0.2, 5.0),
    }


def operate(field, screening, wt, wy, wx):
    before_time = jnp.roll(wt, 1, axis=0)
    before_row = jnp.roll(wy, 1, axis=1)
    before_col = jnp.roll(wx, 1, axis=2)
    total = screening * field
    total = total + wt * (field - jnp.roll(field, -1, axis=1))
    total = total + before_time * (field - jnp.roll(field, 1, axis=1))
    total = total + wy * (field - jnp.roll(field, -1, axis=2))
    total = total + before_row * (field - jnp.roll(field, 1, axis=2))
    total = total + wx * (field - jnp.roll(field, -1, axis=3))
    total = total + before_col * (field - jnp.roll(field, 1, axis=3))
    return total


def channel_sum(left, right):
    return jnp.sum(left * right, axis=(1, 2, 3))


def expand(scalar):
    return scalar[:, None, None, None]


def reference(right_side, screening, time_weight, row_weight, column_weight):
    wy = row_weight.at[:, -1, :].set(0.0)
    wx = column_weight.at[:, :, -1].set(0.0)
    wt = time_weight
    solution_field = jnp.zeros_like(right_side)
    residual = right_side
    direction = right_side
    norm_now = channel_sum(residual, residual)
    for step in range(ITERS):
        image = operate(direction, screening, wt, wy, wx)
        alpha = norm_now / channel_sum(direction, image)
        solution_field = solution_field + expand(alpha) * direction
        residual = residual - expand(alpha) * image
        norm_next = channel_sum(residual, residual)
        direction = residual + expand(norm_next / norm_now) * direction
        norm_now = norm_next
    return solution_field, residual
```

```python
import functools

import jax
import jax.numpy as jnp
from jax import lax
from jax.experimental import pallas as pl
from jax.experimental.pallas import tpu as pltpu
from jax.sharding import PartitionSpec as P

MESH = pl.DeviceIdType.MESH
LANES = 128


def kernel(sizes, b, s, wt, wy, wx, x_out, r_out,
           bv, sv, wtv, wyv, wxv, byv, bxv, av, rv, pv, qv,
           hz, hwt, srow, hrow, hcol, hwx, xo, ro, part1, part2,
           load_sem, z_send, z_recv, wt_send, wt_recv, row_send, row_recv,
           col_send, col_recv, wx_send, wx_recv, sum1_send, sum1_recv,
           sum2_send, sum2_recv, out_sem):
    tms, bands, strips = sizes
    chans, frames, rows, cols = b.shape
    me_t, me_r, me_c = (lax.axis_index(a) for a in ("tm", "row", "col"))
    up_t, down_t = lax.rem(me_t + 1, tms), lax.rem(me_t + tms - 1, tms)
    up_r, down_r = lax.rem(me_r + 1, bands), lax.rem(me_r + bands - 1, bands)
    up_c, down_c = lax.rem(me_c + 1, strips), lax.rem(me_c + strips - 1, strips)
    sends = []

    def send(src, dst, ss, rs, **where):
        copy = pltpu.make_async_remote_copy(
            src_ref=src, dst_ref=dst, send_sem=ss, recv_sem=rs,
            device_id=where, device_id_type=MESH)
        copy.start()
        sends.append(copy)
        return copy

    loads = [pltpu.make_async_copy(h, v, load_sem.at[i]) for i, (h, v) in enumerate(
        ((b, bv), (wy, wyv), (wx, wxv), (s, sv), (wt, wtv)))]
    for copy in loads:
        copy.start()

    group = [(i, j) for i in range(bands) for j in range(strips) if i or j]
    barrier = pltpu.get_barrier_semaphore()
    for d in range(1, tms):
        pl.semaphore_signal(barrier, inc=1, device_id={"tm": lax.rem(me_t + d, tms)}, device_id_type=MESH)
    for i, j in group:
        pl.semaphore_signal(barrier, inc=1, device_id={
            "row": lax.rem(me_r + i, bands), "col": lax.rem(me_c + j, strips)}, device_id_type=MESH)
    pl.semaphore_wait(barrier, tms - 1 + len(group))

    def send_time(phase, c, field):
        up = send(field.at[c, frames - 1], hz.at[phase, 0, c], z_send.at[phase, 0, c], z_recv.at[phase, 0, c], tm=up_t)
        down = send(field.at[c, 0], hz.at[phase, 1, c], z_send.at[phase, 1, c], z_recv.at[phase, 1, c], tm=down_t)
        return [up, down]

    def send_side(phase, c, field):
        for f in range(frames):
            srow[phase, 0, c, f:f + 1, :] = field[c, f, rows - 1:rows, :]
            srow[phase, 1, c, f:f + 1, :] = field[c, f, 0:1, :]
            if phase == 0 and c == 0:
                srow[phase, 0, c, frames + f:frames + f + 1, :] = wyv[f, rows - 1:rows, :]
        return [
            send(srow.at[phase, 0, c], hrow.at[phase, 0, c], row_send.at[phase, 0, c], row_recv.at[phase, 0, c], row=up_r),
            send(srow.at[phase, 1, c], hrow.at[phase, 1, c], row_send.at[phase, 1, c], row_recv.at[phase, 1, c], row=down_r),
            send(field.at[c, :, :, cols - LANES:], hcol.at[phase, 0, c], col_send.at[phase, 0, c], col_recv.at[phase, 0, c], col=up_c),
            send(field.at[c, :, :, :LANES], hcol.at[phase, 1, c], col_send.at[phase, 1, c], col_recv.at[phase, 1, c], col=down_c),
        ]

    wait_b = {}
    weight = send(wt.at[frames - 1], hwt, wt_send, wt_recv, tm=up_t)
    for c in range(chans):
        wait_b[c] = send_time(0, c, b)

    row_ids = lax.broadcasted_iota(jnp.int32, (rows, cols), 0)
    lane_ids = lax.broadcasted_iota(jnp.int32, (rows, LANES), 1)
    last_band = me_r == bands - 1
    last_strip = me_c == strips - 1
    for copy in loads[:3]:
        copy.wait()
    for f in range(frames):
        wyv[f, rows - 1:rows, :] = jnp.where(last_band, 0.0, wyv[f, rows - 1:rows, :])
        tile = wxv[f, :, cols - LANES:]
        wxv[f, :, cols - LANES:] = jnp.where(jnp.logical_and(last_strip, lane_ids == LANES - 1), 0.0, tile)
    strip = send(wxv.at[:, :, cols - LANES:], hwx, wx_send, wx_recv, col=up_c)
    for c in range(chans):
        wait_b[c] += send_side(0, c, bv)

    def before_row(value, rim):
        return jnp.where(row_ids == 0, rim, pltpu.roll(value, 1, 0))

    def after_row(value, rim):
        return jnp.where(row_ids == rows - 1, rim, pltpu.roll(value, rows - 1, 0))

    def before_col(value, rim):
        moved = pltpu.roll(value, 1, 1)
        edge = jnp.where(lane_ids == 0, pltpu.roll(rim, 1, 1), moved[:, :LANES])
        return jnp.concatenate([edge, moved[:, LANES:]], axis=1)

    def after_col(value, rim):
        moved = pltpu.roll(value, cols - 1, 1)
        edge = jnp.where(lane_ids == LANES - 1, pltpu.roll(rim, LANES - 1, 1), moved[:, cols - LANES:])
        return jnp.concatenate([moved[:, :cols - LANES], edge], axis=1)

    def operate(c, f, field, rim):
        v = field[c, f]
        after = field[c, f + 1] if f < frames - 1 else rim(hz, 1, c)
        prior = field[c, f - 1] if f > 0 else rim(hz, 0, c)
        before_time = wtv[f - 1] if f > 0 else hwt[...]
        one = slice(f, f + 1)
        total = sv[f] * v
        total = total + wtv[f] * (v - after)
        total = total + before_time * (v - prior)
        total = total + wyv[f] * (v - after_row(v, rim(hrow, 1, c, one)))
        total = total + byv[f] * (v - before_row(v, rim(hrow, 0, c, one)))
        total = total + wxv[f] * (v - after_col(v, rim(hcol, 1, c, f)))
        total = total + bxv[f] * (v - before_col(v, rim(hcol, 0, c, f)))
        return total

    tile_rows = lax.broadcasted_iota(jnp.int32, (8, LANES), 0)

    def lanes_sum(value):
        value = jnp.sum(value, axis=0, keepdims=True)
        total = value[:, :LANES]
        for k in range(LANES, cols, LANES):
            total = total + value[:, k:k + LANES]
        return total

    def total_of(k, parts):
        tile = jnp.zeros((8, LANES), jnp.float32)
        for q, value in enumerate(parts):
            tile = jnp.where(tile_rows == q, value, tile)
        mine = me_r * strips + me_c
        part1[k, mine] = tile
        for n, (i, j) in enumerate(group):
            to_r, to_c = lax.rem(me_r + i, bands), lax.rem(me_c + j, strips)
            send(part1.at[k, mine], part1.at[k, mine], sum1_send.at[k, n], sum1_recv.at[k, mine], row=to_r, col=to_c)
        for i, j in group:
            other = lax.rem(me_r + i, bands) * strips + lax.rem(me_c + j, strips)
            pltpu.make_async_copy(part1.at[k, other], part1.at[k, other], sum1_recv.at[k, other]).wait()
        tile = part1[k, 0]
        for n in range(1, bands * strips):
            tile = tile + part1[k, n]
        part2[k, me_t] = tile
        for d in range(1, tms):
            send(part2.at[k, me_t], part2.at[k, me_t], sum2_send.at[k, d], sum2_recv.at[k, me_t], tm=lax.rem(me_t + d, tms))
        for d in range(1, tms):
            other = lax.rem(me_t + d, tms)
            pltpu.make_async_copy(part2.at[k, other], part2.at[k, other], sum2_recv.at[k, other]).wait()
        tile = part2[k, 0]
        for n in range(1, tms):
            tile = tile + part2[k, n]
        return jnp.sum(tile, axis=1, keepdims=True)

    def plain(ref, *index):
        return ref[(0,) + index]

    for copy in loads[3:]:
        copy.wait()
    weight.wait_recv()
    strip.wait_recv()
    wait_a, squares, products = {}, [], []
    for c in range(chans):
        for copy in wait_b[c]:
            copy.wait_recv()
        if c == 0:
            for f in range(frames):
                byv[f] = before_row(wyv[f], hrow[0, 0, 0, frames + f:frames + f + 1])
                bxv[f] = before_col(wxv[f], hwx[f])
        square, product = 0.0, 0.0
        for f in range(frames):
            image = operate(c, f, bv, plain)
            av[c, f] = image
            square = square + bv[c, f] * bv[c, f]
            product = product + bv[c, f] * image
        wait_a[c] = send_time(1, c, av) + send_side(1, c, av)
        squares.append(lanes_sum(square))
        products.append(lanes_sum(product))

    sums = total_of(0, squares + products)
    norm0 = [sums[c:c + 1] for c in range(chans)]
    alpha0 = [sums[c:c + 1] / sums[chans + c:chans + c + 1] for c in range(chans)]
    squares = []
    for c in range(chans):
        square = 0.0
        for f in range(frames):
            residual = bv[c, f] - alpha0[c] * av[c, f]
            rv[c, f] = residual
            square = square + residual * residual
        squares.append(lanes_sum(square))
    sums = total_of(1, squares)
    norm1 = [sums[c:c + 1] for c in range(chans)]
    beta = [norm1[c] / norm0[c] for c in range(chans)]

    def combined(ref, side, c, *index):
        own = ref[(0, side, c) + index]
        return (own - alpha0[c] * ref[(1, side, c) + index]) + beta[c] * own

    for c in range(chans):
        for f in range(frames):
            pv[c, f] = rv[c, f] + beta[c] * bv[c, f]
    products = []
    for c in range(chans):
        for copy in wait_a[c]:
            copy.wait_recv()
        product = 0.0
        for f in range(frames):
            image = operate(c, f, pv, combined)
            qv[c, f] = image
            product = product + pv[c, f] * image
        products.append(lanes_sum(product))
    sums = total_of(2, products)
    outs = []
    for c in range(chans):
        alpha1 = norm1[c] / sums[c:c + 1]
        for f in range(frames):
            xo[c, f] = alpha0[c] * bv[c, f] + alpha1 * pv[c, f]
            ro[c, f] = rv[c, f] - alpha1 * qv[c, f]
        for i, (v, h) in enumerate(((xo, x_out), (ro, r_out))):
            copy = pltpu.make_async_copy(v.at[c], h.at[c], out_sem.at[i, c])
            copy.start()
            outs.append(copy)
    for copy in sends:
        copy.wait_send()
    for copy in outs:
        copy.wait()


def shards(sizes, right_side, screening, time_weight, row_weight, column_weight):
    tms, bands, strips = sizes
    chans, frames, rows, cols = right_side.shape
    f32 = jnp.float32
    field = pltpu.VMEM((chans, frames, rows, cols), f32)
    coefficient = pltpu.VMEM((frames, rows, cols), f32)
    tall = -(-2 * frames // 8) * 8
    dma = pltpu.SemaphoreType.DMA
    anywhere = pl.BlockSpec(memory_space=pl.ANY)
    shape = jax.ShapeDtypeStruct(right_side.shape, f32)
    return pl.pallas_call(
        functools.partial(kernel, sizes),
        out_shape=(shape, shape),
        in_specs=[anywhere] * 5,
        out_specs=(anywhere, anywhere),
        scratch_shapes=[field] + [coefficient] * 6 + [field] * 4 + [
            pltpu.VMEM((2, 2, chans, rows, cols), f32),
            pltpu.VMEM((rows, cols), f32),
            pltpu.VMEM((2, 2, chans, tall, cols), f32),
            pltpu.VMEM((2, 2, chans, tall, cols), f32),
            pltpu.VMEM((2, 2, chans, frames, rows, LANES), f32),
            pltpu.VMEM((frames, rows, LANES), f32),
            field, field,
            pltpu.VMEM((3, bands * strips, 8, LANES), f32),
            pltpu.VMEM((3, tms, 8, LANES), f32),
            dma((5,)),
            dma((2, 2, chans)), dma((2, 2, chans)), dma, dma,
            dma((2, 2, chans)), dma((2, 2, chans)),
            dma((2, 2, chans)), dma((2, 2, chans)), dma, dma,
            dma((3, bands * strips)), dma((3, bands * strips)),
            dma((3, tms)), dma((3, tms)),
            dma((2, chans)),
        ],
        compiler_params=pltpu.CompilerParams(
            collective_id=0, has_side_effects=True, vmem_limit_bytes=24 * 1024 * 1024),
        cost_estimate=pl.CostEstimate(flops=10_000_000, bytes_accessed=2_000_000, transcendentals=0),
    )(right_side, screening, time_weight, row_weight, column_weight)


def solution(mesh):
    field = P(None, ("clip", "tm"), "row", "col")
    coefficient = P(("clip", "tm"), "row", "col")
    sizes = tuple(mesh.shape[a] for a in ("tm", "row", "col"))
    return jax.shard_map(
        functools.partial(shards, sizes),
        mesh=mesh,
        in_specs=(field,) + (coefficient,) * 4,
        out_specs=(field, field),
        check_vma=False,
    )
```

```python
import functools

import jax
import jax.numpy as jnp
from jax import lax
from jax.experimental import pallas as pl
from jax.experimental.pallas import tpu as pltpu
from jax.sharding import PartitionSpec as P

MESH = pl.DeviceIdType.MESH
LANES = 128
VMEM_BYTES = 60 * 1024 * 1024


def kernel(sizes, b, s, wt, wy, wx, x_out, r_out,
           bv, sv, wtv, wyv, wxv, byv, bxv, av, rv, pv, qv,
           hz, hwt, srow, hrow, hcol, hwx, part,
           load_sem, z_send, z_recv, wt_send, wt_recv, row_send, row_recv,
           col_send, col_recv, wx_send, wx_recv, sum_send, sum_recv):
    tms, bands, strips = sizes
    chans, frames, rows, cols = b.shape
    half = rows // 2
    me_t, me_r, me_c = (lax.axis_index(a) for a in ("tm", "row", "col"))
    up_t, down_t = lax.rem(me_t + 1, tms), lax.rem(me_t + tms - 1, tms)
    up_r, down_r = lax.rem(me_r + 1, bands), lax.rem(me_r + bands - 1, bands)
    up_c, down_c = lax.rem(me_c + 1, strips), lax.rem(me_c + strips - 1, strips)
    sends = []

    def send(src, dst, ss, rs, **where):
        copy = pltpu.make_async_remote_copy(
            src_ref=src, dst_ref=dst, send_sem=ss, recv_sem=rs,
            device_id=where, device_id_type=MESH)
        copy.start()
        sends.append(copy)
        return copy

    loads = [pltpu.make_async_copy(h, v, load_sem.at[i]) for i, (h, v) in enumerate(
        ((b, bv), (wy, wyv), (wx, wxv), (s, sv), (wt, wtv)))]
    for copy in loads:
        copy.start()

    group = []
    for t in range(tms):
        for i in range(bands):
            for j in range(strips):
                if t or i or j:
                    where = (lax.rem(me_t + t, tms), lax.rem(me_r + i, bands), lax.rem(me_c + j, strips))
                    group.append((dict(zip(("tm", "row", "col"), where)), (where[0] * bands + where[1]) * strips + where[2]))
    mine = (me_t * bands + me_r) * strips + me_c
    barrier = pltpu.get_barrier_semaphore()
    for where, _ in group:
        pl.semaphore_signal(barrier, inc=1, device_id=where, device_id_type=MESH)
    pl.semaphore_wait(barrier, len(group))

    def send_time(phase, c, field, early):
        n = 1 - early
        fore = pl.ds(n * half, half)
        back = pl.ds((1 - n) * half, half)
        return [
            send(field.at[c, frames - 1, fore], hz.at[phase, 0, c, fore], z_send.at[phase, 0, c, n], z_recv.at[phase, 0, c, n], tm=up_t),
            send(field.at[c, 0, back], hz.at[phase, 1, c, back], z_send.at[phase, 1, c, n], z_recv.at[phase, 1, c, n], tm=down_t),
        ]

    def send_frames(c, field):
        return [
            send(field.at[c, frames - 1], hz.at[0, 0, c], z_send.at[0, 0, c, 0], z_recv.at[0, 0, c, 0], tm=up_t),
            send(field.at[c, 0], hz.at[0, 1, c], z_send.at[0, 1, c, 0], z_recv.at[0, 1, c, 0], tm=down_t),
        ]

    def send_side(phase, c, field):
        for f in range(frames):
            srow[phase, 0, c, f:f + 1, :] = field[c, f, rows - 1:rows, :]
            srow[phase, 1, c, f:f + 1, :] = field[c, f, 0:1, :]
            if phase == 0 and c == 0:
                srow[phase, 0, c, frames + f:frames + f + 1, :] = wyv[f, rows - 1:rows, :]
        return [
            send(srow.at[phase, 0, c], hrow.at[phase, 0, c], row_send.at[phase, 0, c], row_recv.at[phase, 0, c], row=up_r),
            send(srow.at[phase, 1, c], hrow.at[phase, 1, c], row_send.at[phase, 1, c], row_recv.at[phase, 1, c], row=down_r),
            send(field.at[c, :, :, cols - LANES:], hcol.at[phase, 0, c], col_send.at[phase, 0, c], col_recv.at[phase, 0, c], col=up_c),
            send(field.at[c, :, :, :LANES], hcol.at[phase, 1, c], col_send.at[phase, 1, c], col_recv.at[phase, 1, c], col=down_c),
        ]

    wait_b = {}
    weight = send(wt.at[frames - 1], hwt, wt_send, wt_recv, tm=up_t)
    for c in range(chans):
        wait_b[c] = send_frames(c, b)

    row_ids = lax.broadcasted_iota(jnp.int32, (rows, cols), 0)
    lane_ids = lax.broadcasted_iota(jnp.int32, (rows, LANES), 1)
    last_band = me_r == bands - 1
    last_strip = me_c == strips - 1
    for copy in loads[:3]:
        copy.wait()
    for f in range(frames):
        wyv[f, rows - 1:rows, :] = jnp.where(last_band, 0.0, wyv[f, rows - 1:rows, :])
        tile = wxv[f, :, cols - LANES:]
        wxv[f, :, cols - LANES:] = jnp.where(jnp.logical_and(last_strip, lane_ids == LANES - 1), 0.0, tile)
    strip = send(wxv.at[:, :, cols - LANES:], hwx, wx_send, wx_recv, col=up_c)
    for c in range(chans):
        wait_b[c] += send_side(0, c, bv)

    def before_row(value, rim):
        return jnp.where(row_ids == 0, rim, pltpu.roll(value, 1, 0))

    def after_row(value, rim):
        return jnp.where(row_ids == rows - 1, rim, pltpu.roll(value, rows - 1, 0))

    def before_col(value, rim):
        moved = pltpu.roll(value, 1, 1)
        edge = jnp.where(lane_ids == 0, pltpu.roll(rim, 1, 1), moved[:, :LANES])
        return jnp.concatenate([edge, moved[:, LANES:]], axis=1)

    def after_col(value, rim):
        moved = pltpu.roll(value, cols - 1, 1)
        edge = jnp.where(lane_ids == LANES - 1, pltpu.roll(rim, LANES - 1, 1), moved[:, cols - LANES:])
        return jnp.concatenate([moved[:, :cols - LANES], edge], axis=1)

    def inner(c, f, field, rim):
        v = field[c, f]
        one = slice(f, f + 1)
        total = sv[f] * v
        if f < frames - 1:
            total = total + wtv[f] * (v - field[c, f + 1])
        if f > 0:
            total = total + wtv[f - 1] * (v - field[c, f - 1])
        total = total + wyv[f] * (v - after_row(v, rim(hrow, 1, c, one)))
        total = total + byv[f] * (v - before_row(v, rim(hrow, 0, c, one)))
        total = total + wxv[f] * (v - after_col(v, rim(hcol, 1, c, f)))
        total = total + bxv[f] * (v - before_col(v, rim(hcol, 0, c, f)))
        return total

    def outer(c, f, field, rim):
        total = 0.0
        if f == 0:
            total = total + hwt[...] * (field[c, f] - rim(hz, 0, c))
        if f == frames - 1:
            total = total + wtv[f] * (field[c, f] - rim(hz, 1, c))
        return total

    def whole_sum(value):
        return jnp.sum(jnp.sum(value, axis=0, keepdims=True), axis=1, keepdims=True)

    row_lanes = lax.broadcasted_iota(jnp.int32, (1, LANES), 1)

    def exchange(k, values):
        line = jnp.zeros((1, LANES), jnp.float32)
        for (q, c), value in values.items():
            line = jnp.where(row_lanes == 8 * q + c, value, line)
        part[k, mine] = line
        copies = [send(part.at[k, mine], part.at[k, mine], sum_send.at[k, n], sum_recv.at[k, mine], **where)
                  for n, (where, _) in enumerate(group)]
        return copies

    def collect(k):
        for _, other in group:
            pltpu.make_async_copy(part.at[k, other], part.at[k, other], sum_recv.at[k, other]).wait()
        return jnp.concatenate([part[k, n] for n in range(tms * bands * strips)], axis=0)

    def plain(ref, *index):
        return ref[(0,) + index]

    for copy in loads[3:]:
        copy.wait()
    weight.wait_recv()
    strip.wait_recv()
    wait_side, wait_early, wait_late, values = {}, {}, {}, {}
    for c in range(chans):
        for copy in wait_b[c]:
            copy.wait_recv()
        if c == 0:
            for f in range(frames):
                byv[f] = before_row(wyv[f], hrow[0, 0, 0, frames + f:frames + f + 1])
                bxv[f] = before_col(wxv[f], hwx[f])
        m0, m1, m2 = 0.0, 0.0, 0.0
        for f in range(frames):
            image = inner(c, f, bv, plain) + outer(c, f, bv, plain)
            av[c, f] = image
            m0 = m0 + bv[c, f] * bv[c, f]
            m1 = m1 + bv[c, f] * image
            m2 = m2 + image * image
        wait_early[c] = send_time(1, c, av, True)
        if c == 0:
            wait_late[c] = send_time(1, c, av, False)
        wait_side[c] = send_side(1, c, av)
        if c == chans - 1:
            for other in range(1, chans):
                wait_late[other] = send_time(1, other, av, False)
        m0, m1, m2 = whole_sum(m0), whole_sum(m1), whole_sum(m2)
        share = jnp.where(m2 > 0.0, m1 / jnp.where(m2 > 0.0, m2, 1.0), 0.0)
        e0, e1 = 0.0, 0.0
        for f in range(frames):
            rest = bv[c, f] - share * av[c, f]
            e0 = e0 + rest * rest
            e1 = e1 + rest * av[c, f]
        for q, value in enumerate((m0, m1, m2, share, whole_sum(e0), whole_sum(e1))):
            values[q, c] = value
    exchange(0, values)

    every = collect(0)
    totals = jnp.sum(every, axis=0, keepdims=True)

    def taken(value, q):
        return pltpu.roll(value, LANES - 8 * q, 1)

    steps = totals / taken(totals, 1)
    gap = steps - taken(every, 3)
    norms = jnp.sum(taken(every, 4) + gap * (gap * taken(every, 2) - 2.0 * taken(every, 5)), axis=0, keepdims=True)
    ratios = norms / totals
    alpha0 = [steps[:, c:c + 1] for c in range(chans)]
    norm1 = [norms[:, c:c + 1] for c in range(chans)]
    beta = [ratios[:, c:c + 1] for c in range(chans)]

    def combined(ref, side, c, *index):
        own = ref[(0, side, c) + index]
        return (own - alpha0[c] * ref[(1, side, c) + index]) + beta[c] * own

    products = []
    for c in range(chans):
        for f in range(frames):
            residual = bv[c, f] - alpha0[c] * av[c, f]
            rv[c, f] = residual
            pv[c, f] = residual + beta[c] * bv[c, f]
        for copy in wait_side[c]:
            copy.wait_recv()
        product = 0.0
        for f in range(frames):
            image = inner(c, f, pv, lambda ref, *index: combined(ref, *index))
            qv[c, f] = image
            product = product + pv[c, f] * image
        products.append(product[:half] + product[half:])
    for c in range(chans):
        for copy in wait_early[c]:
            copy.wait_recv()
        upper, lower = slice(0, half), slice(half, rows)
        prior = pv[c, 0, upper] - combined(hz, 0, c, upper)
        after = pv[c, frames - 1, lower] - combined(hz, 1, c, lower)
        products[c] = products[c] + hwt[upper] * prior * prior + wtv[frames - 1, lower] * after * after
    exchange(1, {(0, c): whole_sum(products[c]) for c in range(chans)})
    for c in range(chans):
        for copy in wait_late[c]:
            copy.wait_recv()
        for f in sorted({0, frames - 1}):
            qv[c, f] = qv[c, f] + outer(c, f, pv, combined)
    curvatures = jnp.sum(collect(1), axis=0, keepdims=True)
    for c in range(chans):
        alpha1 = norm1[c] / curvatures[:, c:c + 1]
        for f in range(frames):
            x_out[c, f] = alpha0[c] * bv[c, f] + alpha1 * pv[c, f]
            r_out[c, f] = rv[c, f] - alpha1 * qv[c, f]
    for copy in sends:
        copy.wait_send()


def shards(sizes, right_side, screening, time_weight, row_weight, column_weight):
    tms, bands, strips = sizes
    chans, frames, rows, cols = right_side.shape
    f32 = jnp.float32
    field = pltpu.VMEM((chans, frames, rows, cols), f32)
    coefficient = pltpu.VMEM((frames, rows, cols), f32)
    tall = -(-2 * frames // 8) * 8
    devices = tms * bands * strips
    dma = pltpu.SemaphoreType.DMA
    anywhere = pl.BlockSpec(memory_space=pltpu.HBM)
    inside = pl.BlockSpec(memory_space=pltpu.VMEM)
    shape = jax.ShapeDtypeStruct(right_side.shape, f32)
    return pl.pallas_call(
        functools.partial(kernel, sizes),
        out_shape=(shape, shape),
        in_specs=[anywhere] * 5,
        out_specs=(inside, inside),
        scratch_shapes=[field] + [coefficient] * 6 + [field] * 4 + [
            pltpu.VMEM((2, 2, chans, rows, cols), f32),
            pltpu.VMEM((rows, cols), f32),
            pltpu.VMEM((2, 2, chans, tall, cols), f32),
            pltpu.VMEM((2, 2, chans, tall, cols), f32),
            pltpu.VMEM((2, 2, chans, frames, rows, LANES), f32),
            pltpu.VMEM((frames, rows, LANES), f32),
            pltpu.VMEM((2, devices, 1, LANES), f32),
            dma((5,)),
            dma((2, 2, chans, 2)), dma((2, 2, chans, 2)), dma, dma,
            dma((2, 2, chans)), dma((2, 2, chans)),
            dma((2, 2, chans)), dma((2, 2, chans)), dma, dma,
            dma((2, devices)), dma((2, devices)),
        ],
        compiler_params=pltpu.CompilerParams(
            collective_id=0, has_side_effects=True, vmem_limit_bytes=VMEM_BYTES),
        cost_estimate=pl.CostEstimate(flops=10_000_000, bytes_accessed=2_000_000, transcendentals=0),
    )(right_side, screening, time_weight, row_weight, column_weight)


def solution(mesh):
    field = P(None, ("clip", "tm"), "row", "col")
    coefficient = P(("clip", "tm"), "row", "col")
    sizes = tuple(mesh.shape[a] for a in ("tm", "row", "col"))
    return jax.shard_map(
        functools.partial(shards, sizes),
        mesh=mesh,
        in_specs=(field,) + (coefficient,) * 4,
        out_specs=(field, field),
        check_vma=False,
    )
```

```python
import functools

import jax
import jax.numpy as jnp
from jax import lax
from jax.experimental import pallas as pl
from jax.experimental.pallas import tpu as pltpu
from jax.sharding import PartitionSpec as P

MESH = pl.DeviceIdType.MESH
LANES = 128
VMEM_BYTES = 60 * 1024 * 1024


def kernel(sizes, b, s, wt, wy, wx, x_out, r_out,
           bv, sv, wtv, wyv, wxv, byv, bxv, av, rv, pv, qv,
           hz, hwt, srow, hrow, hcol, hwx, part,
           load_sem, z_send, z_recv, wt_send, wt_recv, row_send, row_recv,
           col_send, col_recv, wx_send, wx_recv, sum_send, sum_recv):
    tms, bands, strips = sizes
    chans, frames, rows, cols = b.shape
    half = rows // 2
    me_t, me_r, me_c = (lax.axis_index(a) for a in ("tm", "row", "col"))
    up_t, down_t = lax.rem(me_t + 1, tms), lax.rem(me_t + tms - 1, tms)
    up_r, down_r = lax.rem(me_r + 1, bands), lax.rem(me_r + bands - 1, bands)
    up_c, down_c = lax.rem(me_c + 1, strips), lax.rem(me_c + strips - 1, strips)
    sends = []

    def send(src, dst, ss, rs, **where):
        copy = pltpu.make_async_remote_copy(
            src_ref=src, dst_ref=dst, send_sem=ss, recv_sem=rs,
            device_id=where, device_id_type=MESH)
        copy.start()
        sends.append(copy)
        return copy

    loads = [pltpu.make_async_copy(h, v, load_sem.at[i]) for i, (h, v) in enumerate(
        ((b, bv), (wy, wyv), (wx, wxv), (s, sv), (wt, wtv)))]
    for copy in loads:
        copy.start()

    group = []
    for t in range(tms):
        for i in range(bands):
            for j in range(strips):
                if t or i or j:
                    where = (lax.rem(me_t + t, tms), lax.rem(me_r + i, bands), lax.rem(me_c + j, strips))
                    group.append((dict(zip(("tm", "row", "col"), where)), (where[0] * bands + where[1]) * strips + where[2]))
    mine = (me_t * bands + me_r) * strips + me_c
    barrier = pltpu.get_barrier_semaphore()
    for where, _ in group:
        pl.semaphore_signal(barrier, inc=1, device_id=where, device_id_type=MESH)
    pl.semaphore_wait(barrier, len(group))

    def send_time(phase, c, field, early):
        n = 1 - early
        fore = pl.ds(n * half, half)
        back = pl.ds((1 - n) * half, half)
        return [
            send(field.at[c, frames - 1, fore], hz.at[phase, 0, c, fore], z_send.at[phase, 0, c, n], z_recv.at[phase, 0, c, n], tm=up_t),
            send(field.at[c, 0, back], hz.at[phase, 1, c, back], z_send.at[phase, 1, c, n], z_recv.at[phase, 1, c, n], tm=down_t),
        ]

    def send_frames(c, field):
        return [
            send(field.at[c, frames - 1], hz.at[0, 0, c], z_send.at[0, 0, c, 0], z_recv.at[0, 0, c, 0], tm=up_t),
            send(field.at[c, 0], hz.at[0, 1, c], z_send.at[0, 1, c, 0], z_recv.at[0, 1, c, 0], tm=down_t),
        ]

    def send_side(phase, c, field):
        for f in range(frames):
            srow[phase, 0, c, f:f + 1, :] = field[c, f, rows - 1:rows, :]
            srow[phase, 1, c, f:f + 1, :] = field[c, f, 0:1, :]
            if phase == 0 and c == 0:
                srow[phase, 0, c, frames + f:frames + f + 1, :] = wyv[f, rows - 1:rows, :]
        return [
            send(srow.at[phase, 0, c], hrow.at[phase, 0, c], row_send.at[phase, 0, c], row_recv.at[phase, 0, c], row=up_r),
            send(srow.at[phase, 1, c], hrow.at[phase, 1, c], row_send.at[phase, 1, c], row_recv.at[phase, 1, c], row=down_r),
            send(field.at[c, :, :, cols - LANES:], hcol.at[phase, 0, c], col_send.at[phase, 0, c], col_recv.at[phase, 0, c], col=up_c),
            send(field.at[c, :, :, :LANES], hcol.at[phase, 1, c], col_send.at[phase, 1, c], col_recv.at[phase, 1, c], col=down_c),
        ]

    wait_b = {}
    weight = send(wt.at[frames - 1], hwt, wt_send, wt_recv, tm=up_t)
    for c in range(chans):
        wait_b[c] = send_frames(c, b)

    row_ids = lax.broadcasted_iota(jnp.int32, (rows, cols), 0)
    lane_ids = lax.broadcasted_iota(jnp.int32, (rows, LANES), 1)
    last_band = me_r == bands - 1
    last_strip = me_c == strips - 1
    for copy in loads[:3]:
        copy.wait()
    for f in range(frames):
        wyv[f, rows - 1:rows, :] = jnp.where(last_band, 0.0, wyv[f, rows - 1:rows, :])
        tile = wxv[f, :, cols - LANES:]
        wxv[f, :, cols - LANES:] = jnp.where(jnp.logical_and(last_strip, lane_ids == LANES - 1), 0.0, tile)
    strip = send(wxv.at[:, :, cols - LANES:], hwx, wx_send, wx_recv, col=up_c)
    for c in range(chans):
        wait_b[c] += send_side(0, c, bv)

    def before_row(value, rim):
        return jnp.where(row_ids == 0, rim, pltpu.roll(value, 1, 0))

    def after_row(value, rim):
        return jnp.where(row_ids == rows - 1, rim, pltpu.roll(value, rows - 1, 0))

    def before_col(value, rim):
        moved = pltpu.roll(value, 1, 1)
        edge = jnp.where(lane_ids == 0, pltpu.roll(rim, 1, 1), moved[:, :LANES])
        return jnp.concatenate([edge, moved[:, LANES:]], axis=1)

    def after_col(value, rim):
        moved = pltpu.roll(value, cols - 1, 1)
        edge = jnp.where(lane_ids == LANES - 1, pltpu.roll(rim, LANES - 1, 1), moved[:, cols - LANES:])
        return jnp.concatenate([moved[:, :cols - LANES], edge], axis=1)

    def inner(c, f, field, rim):
        v = field[c, f]
        one = slice(f, f + 1)
        total = sv[f] * v
        if f < frames - 1:
            total = total + wtv[f] * (v - field[c, f + 1])
        if f > 0:
            total = total + wtv[f - 1] * (v - field[c, f - 1])
        total = total + wyv[f] * (v - after_row(v, rim(hrow, 1, c, one)))
        total = total + byv[f] * (v - before_row(v, rim(hrow, 0, c, one)))
        total = total + wxv[f] * (v - after_col(v, rim(hcol, 1, c, f)))
        total = total + bxv[f] * (v - before_col(v, rim(hcol, 0, c, f)))
        return total

    def outer(c, f, field, rim):
        total = 0.0
        if f == 0:
            total = total + hwt[...] * (field[c, f] - rim(hz, 0, c))
        if f == frames - 1:
            total = total + wtv[f] * (field[c, f] - rim(hz, 1, c))
        return total

    def whole_sum(value):
        return jnp.sum(jnp.sum(value, axis=0, keepdims=True), axis=1, keepdims=True)

    row_lanes = lax.broadcasted_iota(jnp.int32, (1, LANES), 1)

    def exchange(k, values):
        line = jnp.zeros((1, LANES), jnp.float32)
        for (q, c), value in values.items():
            line = jnp.where(row_lanes == 8 * q + c, value, line)
        part[k, mine] = line
        copies = [send(part.at[k, mine], part.at[k, mine], sum_send.at[k, n], sum_recv.at[k, mine], **where)
                  for n, (where, _) in enumerate(group)]
        return copies

    def collect(k):
        for _, other in group:
            pltpu.make_async_copy(part.at[k, other], part.at[k, other], sum_recv.at[k, other]).wait()
        return jnp.concatenate([part[k, n] for n in range(tms * bands * strips)], axis=0)

    def plain(ref, *index):
        return ref[(0,) + index]

    for copy in loads[3:]:
        copy.wait()
    weight.wait_recv()
    strip.wait_recv()
    wait_side, wait_early, wait_late, values = {}, {}, {}, {}
    for c in range(chans):
        for copy in wait_b[c]:
            copy.wait_recv()
        if c == 0:
            for f in range(frames):
                byv[f] = before_row(wyv[f], hrow[0, 0, 0, frames + f:frames + f + 1])
                bxv[f] = before_col(wxv[f], hwx[f])
        m0, m1, m2 = 0.0, 0.0, 0.0
        for f in range(frames):
            image = inner(c, f, bv, plain) + outer(c, f, bv, plain)
            av[c, f] = image
            m0 = m0 + bv[c, f] * bv[c, f]
            m1 = m1 + bv[c, f] * image
            m2 = m2 + image * image
        wait_early[c] = send_time(1, c, av, True)
        if c == 0:
            wait_late[c] = send_time(1, c, av, False)
        wait_side[c] = send_side(1, c, av)
        if c == chans - 1:
            for other in range(1, chans):
                wait_late[other] = send_time(1, other, av, False)
        m0, m1, m2 = whole_sum(m0), whole_sum(m1), whole_sum(m2)
        share = jnp.where(m2 > 0.0, m1 / jnp.where(m2 > 0.0, m2, 1.0), 0.0)
        e0, e1 = 0.0, 0.0
        for f in range(frames):
            rest = bv[c, f] - share * av[c, f]
            e0 = e0 + rest * rest
            e1 = e1 + rest * av[c, f]
        for q, value in enumerate((m0, m1, m2, share, whole_sum(e0), whole_sum(e1))):
            values[q, c] = value
    exchange(0, values)

    every = collect(0)
    totals = jnp.sum(every, axis=0, keepdims=True)

    def taken(value, q):
        return pltpu.roll(value, LANES - 8 * q, 1)

    steps = totals / taken(totals, 1)
    gap = steps - taken(every, 3)
    norms = jnp.sum(taken(every, 4) + gap * (gap * taken(every, 2) - 2.0 * taken(every, 5)), axis=0, keepdims=True)
    ratios = norms / totals
    alpha0 = [steps[:, c:c + 1] for c in range(chans)]
    norm1 = [norms[:, c:c + 1] for c in range(chans)]
    beta = [ratios[:, c:c + 1] for c in range(chans)]

    def combined(ref, side, c, *index):
        own = ref[(0, side, c) + index]
        return (own - alpha0[c] * ref[(1, side, c) + index]) + beta[c] * own

    products = []
    for c in range(chans):
        for f in range(frames):
            residual = bv[c, f] - alpha0[c] * av[c, f]
            rv[c, f] = residual
            pv[c, f] = residual + beta[c] * bv[c, f]
        for copy in wait_side[c]:
            copy.wait_recv()
        product = 0.0
        for f in range(frames):
            image = inner(c, f, pv, lambda ref, *index: combined(ref, *index))
            qv[c, f] = image
            product = product + pv[c, f] * image
        products.append(product[:half] + product[half:])
    for c in range(chans):
        for copy in wait_early[c]:
            copy.wait_recv()
        upper, lower = slice(0, half), slice(half, rows)
        prior = pv[c, 0, upper] - combined(hz, 0, c, upper)
        after = pv[c, frames - 1, lower] - combined(hz, 1, c, lower)
        products[c] = products[c] + hwt[upper] * prior * prior + wtv[frames - 1, lower] * after * after
    exchange(1, {(0, c): whole_sum(products[c]) for c in range(chans)})
    for c in range(chans):
        for copy in wait_late[c]:
            copy.wait_recv()
        for f in sorted({0, frames - 1}):
            qv[c, f] = qv[c, f] + outer(c, f, pv, combined)
    curvatures = jnp.sum(collect(1), axis=0, keepdims=True)
    for c in range(chans):
        alpha1 = norm1[c] / curvatures[:, c:c + 1]
        for f in range(frames):
            x_out[c, f] = alpha0[c] * bv[c, f] + alpha1 * pv[c, f]
            r_out[c, f] = rv[c, f] - alpha1 * qv[c, f]
    for copy in sends:
        copy.wait_send()


def written(x, r, x_out, r_out, sem):
    copies = [pltpu.make_async_copy(v, h, sem.at[i]) for i, (v, h) in enumerate(((x, x_out), (r, r_out)))]
    for copy in copies:
        copy.start()
    for copy in copies:
        copy.wait()


def shards(sizes, right_side, screening, time_weight, row_weight, column_weight):
    tms, bands, strips = sizes
    chans, frames, rows, cols = right_side.shape
    f32 = jnp.float32
    field = pltpu.VMEM((chans, frames, rows, cols), f32)
    coefficient = pltpu.VMEM((frames, rows, cols), f32)
    tall = -(-2 * frames // 8) * 8
    devices = tms * bands * strips
    dma = pltpu.SemaphoreType.DMA
    anywhere = pl.BlockSpec(memory_space=pltpu.HBM)
    inside = pl.BlockSpec(memory_space=pltpu.VMEM)
    shape = jax.ShapeDtypeStruct(right_side.shape, f32)
    results = pl.pallas_call(
        functools.partial(kernel, sizes),
        out_shape=(pltpu.VMEM(right_side.shape, f32),) * 2,
        in_specs=[anywhere] * 5,
        out_specs=(inside, inside),
        scratch_shapes=[field] + [coefficient] * 6 + [field] * 4 + [
            pltpu.VMEM((2, 2, chans, rows, cols), f32),
            pltpu.VMEM((rows, cols), f32),
            pltpu.VMEM((2, 2, chans, tall, cols), f32),
            pltpu.VMEM((2, 2, chans, tall, cols), f32),
            pltpu.VMEM((2, 2, chans, frames, rows, LANES), f32),
            pltpu.VMEM((frames, rows, LANES), f32),
            pltpu.VMEM((2, devices, 1, LANES), f32),
            dma((5,)),
            dma((2, 2, chans, 2)), dma((2, 2, chans, 2)), dma, dma,
            dma((2, 2, chans)), dma((2, 2, chans)),
            dma((2, 2, chans)), dma((2, 2, chans)), dma, dma,
            dma((2, devices)), dma((2, devices)),
        ],
        compiler_params=pltpu.CompilerParams(
            collective_id=0, has_side_effects=True, vmem_limit_bytes=VMEM_BYTES),
        cost_estimate=pl.CostEstimate(flops=10_000_000, bytes_accessed=2_000_000, transcendentals=0),
    )(right_side, screening, time_weight, row_weight, column_weight)
    return pl.pallas_call(
        written,
        out_shape=(shape, shape),
        in_specs=[inside] * 2,
        out_specs=(anywhere, anywhere),
        scratch_shapes=[dma((2,))],
    )(*results)


def solution(mesh):
    field = P(None, ("clip", "tm"), "row", "col")
    coefficient = P(("clip", "tm"), "row", "col")
    sizes = tuple(mesh.shape[a] for a in ("tm", "row", "col"))
    return jax.shard_map(
        functools.partial(shards, sizes),
        mesh=mesh,
        in_specs=(field,) + (coefficient,) * 4,
        out_specs=(field, field),
        check_vma=False,
    )
```

```python
import functools

import jax
import jax.numpy as jnp
from jax import lax
from jax.experimental import pallas as pl
from jax.experimental.pallas import tpu as pltpu
from jax.sharding import PartitionSpec as P

MESH = pl.DeviceIdType.MESH
LANES = 128
VMEM_BYTES = 60 * 1024 * 1024


def kernel(sizes, b, s, wt, wy, wx, x_out, r_out,
           bv, sv, wtv, wyv, wxv, byv, bxv, av, rv, pv, qv, iv,
           hz, hwt, srow, hrow, hcol, hwx, part,
           load_sem, z_send, z_recv, wt_send, wt_recv, row_send, row_recv,
           col_send, col_recv, wx_send, wx_recv, sum_send, sum_recv):
    tms, bands, strips = sizes
    chans, frames, rows, cols = b.shape
    half = rows // 2
    me_t, me_r, me_c = (lax.axis_index(a) for a in ("tm", "row", "col"))
    up_t, down_t = lax.rem(me_t + 1, tms), lax.rem(me_t + tms - 1, tms)
    up_r, down_r = lax.rem(me_r + 1, bands), lax.rem(me_r + bands - 1, bands)
    up_c, down_c = lax.rem(me_c + 1, strips), lax.rem(me_c + strips - 1, strips)
    sends = []

    def send(src, dst, ss, rs, **where):
        copy = pltpu.make_async_remote_copy(
            src_ref=src, dst_ref=dst, send_sem=ss, recv_sem=rs,
            device_id=where, device_id_type=MESH)
        copy.start()
        sends.append(copy)
        return copy

    loads = [pltpu.make_async_copy(h, v, load_sem.at[i]) for i, (h, v) in enumerate(
        ((b, bv), (wy, wyv), (wx, wxv), (s, sv), (wt, wtv)))]
    for copy in loads:
        copy.start()

    group = []
    for t in sorted(range(tms), reverse=True):
        for i in sorted(range(bands), reverse=True):
            for j in range(strips):
                if t or i or j:
                    where = (lax.rem(me_t + t, tms), lax.rem(me_r + i, bands), lax.rem(me_c + j, strips))
                    group.append((dict(zip(("tm", "row", "col"), where)), (where[0] * bands + where[1]) * strips + where[2]))
    mine = (me_t * bands + me_r) * strips + me_c
    barrier = pltpu.get_barrier_semaphore()
    for where, _ in group:
        pl.semaphore_signal(barrier, inc=1, device_id=where, device_id_type=MESH)
    pl.semaphore_wait(barrier, len(group))

    def send_time(phase, c, field, early):
        n = 1 - early
        fore = pl.ds(n * half, half)
        back = pl.ds((1 - n) * half, half)
        return [
            send(field.at[c, frames - 1, fore], hz.at[phase, 0, c, fore], z_send.at[phase, 0, c, n], z_recv.at[phase, 0, c, n], tm=up_t),
            send(field.at[c, 0, back], hz.at[phase, 1, c, back], z_send.at[phase, 1, c, n], z_recv.at[phase, 1, c, n], tm=down_t),
        ]

    def send_frames(c, field):
        return [
            send(field.at[c, frames - 1], hz.at[0, 0, c], z_send.at[0, 0, c, 0], z_recv.at[0, 0, c, 0], tm=up_t),
            send(field.at[c, 0], hz.at[0, 1, c], z_send.at[0, 1, c, 0], z_recv.at[0, 1, c, 0], tm=down_t),
        ]

    def send_side(phase, c, field):
        for f in range(frames):
            srow[phase, 0, c, f:f + 1, :] = field[c, f, rows - 1:rows, :]
            srow[phase, 1, c, f:f + 1, :] = field[c, f, 0:1, :]
            if phase == 0 and c == 0:
                srow[phase, 0, c, frames + f:frames + f + 1, :] = wyv[f, rows - 1:rows, :]
        return [
            send(srow.at[phase, 0, c], hrow.at[phase, 0, c], row_send.at[phase, 0, c], row_recv.at[phase, 0, c], row=up_r),
            send(srow.at[phase, 1, c], hrow.at[phase, 1, c], row_send.at[phase, 1, c], row_recv.at[phase, 1, c], row=down_r),
            send(field.at[c, :, :, cols - LANES:], hcol.at[phase, 0, c], col_send.at[phase, 0, c], col_recv.at[phase, 0, c], col=up_c),
            send(field.at[c, :, :, :LANES], hcol.at[phase, 1, c], col_send.at[phase, 1, c], col_recv.at[phase, 1, c], col=down_c),
        ]

    wait_b = {}
    weight = send(wt.at[frames - 1], hwt, wt_send, wt_recv, tm=up_t)
    for c in range(chans):
        wait_b[c] = send_frames(c, b)

    row_ids = lax.broadcasted_iota(jnp.int32, (rows, cols), 0)
    lane_ids = lax.broadcasted_iota(jnp.int32, (rows, LANES), 1)
    last_band = me_r == bands - 1
    last_strip = me_c == strips - 1
    for copy in loads[:3]:
        copy.wait()
    for f in range(frames):
        wyv[f, rows - 1:rows, :] = jnp.where(last_band, 0.0, wyv[f, rows - 1:rows, :])
        tile = wxv[f, :, cols - LANES:]
        wxv[f, :, cols - LANES:] = jnp.where(jnp.logical_and(last_strip, lane_ids == LANES - 1), 0.0, tile)
    strip = send(wxv.at[:, :, cols - LANES:], hwx, wx_send, wx_recv, col=up_c)
    for c in range(chans):
        wait_b[c] += send_side(0, c, bv)

    def before_row(value, rim):
        return jnp.where(row_ids == 0, rim, pltpu.roll(value, 1, 0))

    def after_row(value, rim):
        return jnp.where(row_ids == rows - 1, rim, pltpu.roll(value, rows - 1, 0))

    def before_col(value, rim):
        moved = pltpu.roll(value, 1, 1)
        edge = jnp.where(lane_ids == 0, pltpu.roll(rim, 1, 1), moved[:, :LANES])
        return jnp.concatenate([edge, moved[:, LANES:]], axis=1)

    def after_col(value, rim):
        moved = pltpu.roll(value, cols - 1, 1)
        edge = jnp.where(lane_ids == LANES - 1, pltpu.roll(rim, LANES - 1, 1), moved[:, cols - LANES:])
        return jnp.concatenate([moved[:, :cols - LANES], edge], axis=1)

    def inner(c, f, field, rim):
        v = field[c, f]
        one = slice(f, f + 1)
        total = sv[f] * v
        if f < frames - 1:
            total = total + wtv[f] * (v - field[c, f + 1])
        if f > 0:
            total = total + wtv[f - 1] * (v - field[c, f - 1])
        total = total + wyv[f] * (v - after_row(v, rim(hrow, 1, c, one)))
        total = total + byv[f] * (v - before_row(v, rim(hrow, 0, c, one)))
        total = total + wxv[f] * (v - after_col(v, rim(hcol, 1, c, f)))
        total = total + bxv[f] * (v - before_col(v, rim(hcol, 0, c, f)))
        return total

    def outer(c, f, field, rim):
        total = 0.0
        if f == 0:
            total = total + hwt[...] * (field[c, f] - rim(hz, 0, c))
        if f == frames - 1:
            total = total + wtv[f] * (field[c, f] - rim(hz, 1, c))
        return total

    def whole_sum(value):
        return jnp.sum(jnp.sum(value, axis=0, keepdims=True), axis=1, keepdims=True)

    row_lanes = lax.broadcasted_iota(jnp.int32, (1, LANES), 1)

    def exchange(k, values):
        line = jnp.zeros((1, LANES), jnp.float32)
        for (q, c), value in values.items():
            line = jnp.where(row_lanes == 8 * q + c, value, line)
        part[k, mine] = line
        copies = [send(part.at[k, mine], part.at[k, mine], sum_send.at[k, n], sum_recv.at[k, mine], **where)
                  for n, (where, _) in enumerate(group)]
        return copies

    def collect(k):
        for _, other in group:
            pltpu.make_async_copy(part.at[k, other], part.at[k, other], sum_recv.at[k, other]).wait()
        return jnp.concatenate([part[k, n] for n in range(tms * bands * strips)], axis=0)

    def plain(ref, *index):
        return ref[(0,) + index]

    def second(ref, *index):
        return ref[(1,) + index]

    for copy in loads[3:]:
        copy.wait()
    strip.wait_recv()
    wait_side, wait_early, wait_late, values = {}, {}, {}, {}
    for c in range(chans):
        for copy in wait_b[c][2:]:
            copy.wait_recv()
        if c == 0:
            for f in range(frames):
                byv[f] = before_row(wyv[f], hrow[0, 0, 0, frames + f:frames + f + 1])
                bxv[f] = before_col(wxv[f], hwx[f])
        for f in range(frames):
            iv[c, f] = inner(c, f, bv, plain)
    weight.wait_recv()
    for c in range(chans):
        for copy in wait_b[c][:2]:
            copy.wait_recv()
        for f in range(frames):
            av[c, f] = iv[c, f] + outer(c, f, bv, plain)
        wait_early[c] = send_time(1, c, av, True)
        if c == 0:
            wait_late[c] = send_time(1, c, av, False)
        wait_side[c] = send_side(1, c, av)
        if c == chans - 1:
            for other in range(1, chans):
                wait_late[other] = send_time(1, other, av, False)
        m0, m1, m2 = 0.0, 0.0, 0.0
        for f in range(frames):
            m0 = m0 + bv[c, f] * bv[c, f]
            m1 = m1 + bv[c, f] * av[c, f]
            m2 = m2 + av[c, f] * av[c, f]
        m0, m1, m2 = whole_sum(m0), whole_sum(m1), whole_sum(m2)
        share = jnp.where(m2 > 0.0, m1 / jnp.where(m2 > 0.0, m2, 1.0), 0.0)
        e0, e1 = 0.0, 0.0
        for f in range(frames):
            rest = bv[c, f] - share * av[c, f]
            e0 = e0 + rest * rest
            e1 = e1 + rest * av[c, f]
        for q, value in enumerate((m0, m1, m2, share, whole_sum(e0), whole_sum(e1))):
            values[q, c] = value
    exchange(0, values)
    for c in range(chans):
        for copy in wait_side[c]:
            copy.wait_recv()
        for f in range(frames):
            qv[c, f] = inner(c, f, av, second)

    every = collect(0)
    totals = jnp.sum(every, axis=0, keepdims=True)

    def taken(value, q):
        return pltpu.roll(value, LANES - 8 * q, 1)

    steps = totals / taken(totals, 1)
    gap = steps - taken(every, 3)
    norms = jnp.sum(taken(every, 4) + gap * (gap * taken(every, 2) - 2.0 * taken(every, 5)), axis=0, keepdims=True)
    ratios = norms / totals
    alpha0 = [steps[:, c:c + 1] for c in range(chans)]
    norm1 = [norms[:, c:c + 1] for c in range(chans)]
    beta = [ratios[:, c:c + 1] for c in range(chans)]

    def combined(ref, side, c, *index):
        own = ref[(0, side, c) + index]
        return (own - alpha0[c] * ref[(1, side, c) + index]) + beta[c] * own

    products = []
    for c in range(chans):
        for f in range(frames):
            residual = bv[c, f] - alpha0[c] * av[c, f]
            rv[c, f] = residual
            pv[c, f] = residual + beta[c] * bv[c, f]
        product = 0.0
        for f in range(frames):
            image = (iv[c, f] - alpha0[c] * qv[c, f]) + beta[c] * iv[c, f]
            qv[c, f] = image
            product = product + pv[c, f] * image
        products.append(product[:half] + product[half:])
    for c in range(chans):
        for copy in wait_early[c]:
            copy.wait_recv()
        upper, lower = slice(0, half), slice(half, rows)
        prior = pv[c, 0, upper] - combined(hz, 0, c, upper)
        after = pv[c, frames - 1, lower] - combined(hz, 1, c, lower)
        products[c] = products[c] + hwt[upper] * prior * prior + wtv[frames - 1, lower] * after * after
    before = list(sends)
    exchange(1, {(0, c): whole_sum(products[c]) for c in range(chans)})
    for c in range(chans):
        for copy in wait_late[c]:
            copy.wait_recv()
        for f in sorted({0, frames - 1}):
            qv[c, f] = qv[c, f] + outer(c, f, pv, combined)
    for copy in before:
        copy.wait_send()
    curvatures = jnp.sum(collect(1), axis=0, keepdims=True)
    for c in range(chans):
        alpha1 = norm1[c] / curvatures[:, c:c + 1]
        for f in range(frames):
            x_out[c, f] = alpha0[c] * bv[c, f] + alpha1 * pv[c, f]
            r_out[c, f] = rv[c, f] - alpha1 * qv[c, f]
    for copy in sends[len(before):]:
        copy.wait_send()


def shards(sizes, right_side, screening, time_weight, row_weight, column_weight):
    tms, bands, strips = sizes
    chans, frames, rows, cols = right_side.shape
    f32 = jnp.float32
    field = pltpu.VMEM((chans, frames, rows, cols), f32)
    coefficient = pltpu.VMEM((frames, rows, cols), f32)
    tall = -(-2 * frames // 8) * 8
    devices = tms * bands * strips
    dma = pltpu.SemaphoreType.DMA
    anywhere = pl.BlockSpec(memory_space=pltpu.HBM)
    inside = pl.BlockSpec(memory_space=pltpu.VMEM)
    return pl.pallas_call(
        functools.partial(kernel, sizes),
        out_shape=(pltpu.VMEM(right_side.shape, f32),) * 2,
        in_specs=[anywhere] * 5,
        out_specs=(inside, inside),
        scratch_shapes=[field] + [coefficient] * 6 + [field] * 5 + [
            pltpu.VMEM((2, 2, chans, rows, cols), f32),
            pltpu.VMEM((rows, cols), f32),
            pltpu.VMEM((2, 2, chans, tall, cols), f32),
            pltpu.VMEM((2, 2, chans, tall, cols), f32),
            pltpu.VMEM((2, 2, chans, frames, rows, LANES), f32),
            pltpu.VMEM((frames, rows, LANES), f32),
            pltpu.VMEM((2, devices, 1, LANES), f32),
            dma((5,)),
            dma((2, 2, chans, 2)), dma((2, 2, chans, 2)), dma, dma,
            dma((2, 2, chans)), dma((2, 2, chans)),
            dma((2, 2, chans)), dma((2, 2, chans)), dma, dma,
            dma((2, devices)), dma((2, devices)),
        ],
        compiler_params=pltpu.CompilerParams(
            collective_id=0, has_side_effects=True, vmem_limit_bytes=VMEM_BYTES),
        cost_estimate=pl.CostEstimate(flops=10_000_000, bytes_accessed=2_000_000, transcendentals=0),
    )(right_side, screening, time_weight, row_weight, column_weight)


def solution(mesh):
    field = P(None, ("clip", "tm"), "row", "col")
    coefficient = P(("clip", "tm"), "row", "col")
    sizes = tuple(mesh.shape[a] for a in ("tm", "row", "col"))
    return jax.shard_map(
        functools.partial(shards, sizes),
        mesh=mesh,
        in_specs=(field,) + (coefficient,) * 4,
        out_specs=(field, field),
        check_vma=False,
    )
```

```python
import functools

import jax
import jax.numpy as jnp
from jax import lax
from jax.experimental import pallas as pl
from jax.experimental.pallas import tpu as pltpu
from jax.sharding import PartitionSpec as P

MESH = pl.DeviceIdType.MESH
LANES = 128
VMEM_BYTES = 60 * 1024 * 1024


def kernel(sizes, b, s, wt, wy, wx, x_out, r_out,
           bv, sv, wtv, wyv, wxv, byv, bxv, av, rv, pv, qv, iv,
           hz, hwt, srow, hrow, hcol, hwx, part,
           load_sem, z_send, z_recv, wt_send, wt_recv, row_send, row_recv,
           col_send, col_recv, wx_send, wx_recv, sum_send, sum_recv):
    tms, bands, strips = sizes
    chans, frames, rows, cols = b.shape
    half = rows // 2
    me_t, me_r, me_c = (lax.axis_index(a) for a in ("tm", "row", "col"))
    up_t, down_t = lax.rem(me_t + 1, tms), lax.rem(me_t + tms - 1, tms)
    up_r, down_r = lax.rem(me_r + 1, bands), lax.rem(me_r + bands - 1, bands)
    up_c, down_c = lax.rem(me_c + 1, strips), lax.rem(me_c + strips - 1, strips)
    sends = []

    def send(src, dst, ss, rs, **where):
        copy = pltpu.make_async_remote_copy(
            src_ref=src, dst_ref=dst, send_sem=ss, recv_sem=rs,
            device_id=where, device_id_type=MESH)
        copy.start()
        sends.append(copy)
        return copy

    loads = [pltpu.make_async_copy(h, v, load_sem.at[i]) for i, (h, v) in enumerate(
        ((b, bv), (wy, wyv), (wx, wxv), (s, sv), (wt, wtv)))]
    for copy in loads:
        copy.start()

    group = []
    for t in sorted(range(tms), reverse=True):
        for i in sorted(range(bands), reverse=True):
            for j in range(strips):
                if t or i or j:
                    where = (lax.rem(me_t + t, tms), lax.rem(me_r + i, bands), lax.rem(me_c + j, strips))
                    group.append((dict(zip(("tm", "row", "col"), where)), (where[0] * bands + where[1]) * strips + where[2]))
    mine = (me_t * bands + me_r) * strips + me_c
    barrier = pltpu.get_barrier_semaphore()
    for where, _ in group:
        pl.semaphore_signal(barrier, inc=1, device_id=where, device_id_type=MESH)
    pl.semaphore_wait(barrier, len(group))

    def send_time(phase, c, field, early):
        n = 1 - early
        fore = pl.ds(n * half, half)
        back = pl.ds((1 - n) * half, half)
        return [
            send(field.at[c, frames - 1, fore], hz.at[phase, 0, c, fore], z_send.at[phase, 0, c, n], z_recv.at[phase, 0, c, n], tm=up_t),
            send(field.at[c, 0, back], hz.at[phase, 1, c, back], z_send.at[phase, 1, c, n], z_recv.at[phase, 1, c, n], tm=down_t),
        ]

    def send_frames(c, field):
        return [
            send(field.at[c, frames - 1], hz.at[0, 0, c], z_send.at[0, 0, c, 0], z_recv.at[0, 0, c, 0], tm=up_t),
            send(field.at[c, 0], hz.at[0, 1, c], z_send.at[0, 1, c, 0], z_recv.at[0, 1, c, 0], tm=down_t),
        ]

    def send_side(phase, c, field):
        for f in range(frames):
            srow[phase, 0, c, f:f + 1, :] = field[c, f, rows - 1:rows, :]
            srow[phase, 1, c, f:f + 1, :] = field[c, f, 0:1, :]
            if phase == 0 and c == 0:
                srow[phase, 0, c, frames + f:frames + f + 1, :] = wyv[f, rows - 1:rows, :]
        return [
            send(srow.at[phase, 0, c], hrow.at[phase, 0, c], row_send.at[phase, 0, c], row_recv.at[phase, 0, c], row=up_r),
            send(srow.at[phase, 1, c], hrow.at[phase, 1, c], row_send.at[phase, 1, c], row_recv.at[phase, 1, c], row=down_r),
            send(field.at[c, :, :, cols - LANES:], hcol.at[phase, 0, c], col_send.at[phase, 0, c], col_recv.at[phase, 0, c], col=up_c),
            send(field.at[c, :, :, :LANES], hcol.at[phase, 1, c], col_send.at[phase, 1, c], col_recv.at[phase, 1, c], col=down_c),
        ]

    wait_b = {}
    weight = send(wt.at[frames - 1], hwt, wt_send, wt_recv, tm=up_t)
    for c in range(chans):
        wait_b[c] = send_frames(c, b)

    row_ids = lax.broadcasted_iota(jnp.int32, (rows, cols), 0)
    lane_ids = lax.broadcasted_iota(jnp.int32, (rows, LANES), 1)
    last_band = me_r == bands - 1
    last_strip = me_c == strips - 1
    for copy in loads[:3]:
        copy.wait()
    for f in range(frames):
        wyv[f, rows - 1:rows, :] = jnp.where(last_band, 0.0, wyv[f, rows - 1:rows, :])
        tile = wxv[f, :, cols - LANES:]
        wxv[f, :, cols - LANES:] = jnp.where(jnp.logical_and(last_strip, lane_ids == LANES - 1), 0.0, tile)
    strip = send(wxv.at[:, :, cols - LANES:], hwx, wx_send, wx_recv, col=up_c)
    for c in range(chans):
        wait_b[c] += send_side(0, c, bv)

    def before_row(value, rim):
        return jnp.where(row_ids == 0, rim, pltpu.roll(value, 1, 0))

    def after_row(value, rim):
        return jnp.where(row_ids == rows - 1, rim, pltpu.roll(value, rows - 1, 0))

    def before_col(value, rim):
        moved = pltpu.roll(value, 1, 1)
        edge = jnp.where(lane_ids == 0, pltpu.roll(rim, 1, 1), moved[:, :LANES])
        return jnp.concatenate([edge, moved[:, LANES:]], axis=1)

    def after_col(value, rim):
        moved = pltpu.roll(value, cols - 1, 1)
        edge = jnp.where(lane_ids == LANES - 1, pltpu.roll(rim, LANES - 1, 1), moved[:, cols - LANES:])
        return jnp.concatenate([moved[:, :cols - LANES], edge], axis=1)

    def inner(c, f, field, rim):
        v = field[c, f]
        one = slice(f, f + 1)
        total = sv[f] * v
        if f < frames - 1:
            total = total + wtv[f] * (v - field[c, f + 1])
        if f > 0:
            total = total + wtv[f - 1] * (v - field[c, f - 1])
        total = total + wyv[f] * (v - after_row(v, rim(hrow, 1, c, one)))
        total = total + byv[f] * (v - before_row(v, rim(hrow, 0, c, one)))
        total = total + wxv[f] * (v - after_col(v, rim(hcol, 1, c, f)))
        total = total + bxv[f] * (v - before_col(v, rim(hcol, 0, c, f)))
        return total

    def outer(c, f, field, rim):
        total = 0.0
        if f == 0:
            total = total + hwt[...] * (field[c, f] - rim(hz, 0, c))
        if f == frames - 1:
            total = total + wtv[f] * (field[c, f] - rim(hz, 1, c))
        return total

    def whole_sum(value):
        return jnp.sum(jnp.sum(value, axis=0, keepdims=True), axis=1, keepdims=True)

    row_lanes = lax.broadcasted_iota(jnp.int32, (1, LANES), 1)

    def exchange(k, values):
        line = jnp.zeros((1, LANES), jnp.float32)
        for (q, c), value in values.items():
            line = jnp.where(row_lanes == 8 * q + c, value, line)
        part[k, mine] = line
        copies = [send(part.at[k, mine], part.at[k, mine], sum_send.at[k, n], sum_recv.at[k, mine], **where)
                  for n, (where, _) in enumerate(group)]
        return copies

    def collect(k):
        for _, other in group:
            pltpu.make_async_copy(part.at[k, other], part.at[k, other], sum_recv.at[k, other]).wait()
        return jnp.concatenate([part[k, n] for n in range(tms * bands * strips)], axis=0)

    def plain(ref, *index):
        return ref[(0,) + index]

    def second(ref, *index):
        return ref[(1,) + index]

    for copy in loads[3:]:
        copy.wait()
    strip.wait_recv()
    wait_side, wait_early, wait_late, values = {}, {}, {}, {}
    for c in range(chans):
        for copy in wait_b[c][2:]:
            copy.wait_recv()
        if c == 0:
            for f in range(frames):
                byv[f] = before_row(wyv[f], hrow[0, 0, 0, frames + f:frames + f + 1])
                bxv[f] = before_col(wxv[f], hwx[f])
        for f in range(frames):
            iv[c, f] = inner(c, f, bv, plain)
    weight.wait_recv()
    for c in range(chans):
        for copy in wait_b[c][:2]:
            copy.wait_recv()
        for f in range(frames):
            av[c, f] = iv[c, f] + outer(c, f, bv, plain)
        wait_early[c] = send_time(1, c, av, True)
        wait_side[c] = send_side(1, c, av)
        m0, m1, m2 = 0.0, 0.0, 0.0
        for f in range(frames):
            m0 = m0 + bv[c, f] * bv[c, f]
            m1 = m1 + bv[c, f] * av[c, f]
            m2 = m2 + av[c, f] * av[c, f]
        m0, m1, m2 = whole_sum(m0), whole_sum(m1), whole_sum(m2)
        share = jnp.where(m2 > 0.0, m1 / jnp.where(m2 > 0.0, m2, 1.0), 0.0)
        e0, e1 = 0.0, 0.0
        for f in range(frames):
            rest = bv[c, f] - share * av[c, f]
            e0 = e0 + rest * rest
            e1 = e1 + rest * av[c, f]
        for q, value in enumerate((m0, m1, m2, share, whole_sum(e0), whole_sum(e1))):
            values[q, c] = value
    exchange(0, values)
    for c in range(chans):
        for copy in wait_side[c]:
            copy.wait_recv()
        for f in range(frames):
            qv[c, f] = inner(c, f, av, second)

    for c in range(chans):
        wait_late[c] = send_time(1, c, av, False)
    every = collect(0)
    totals = jnp.sum(every, axis=0, keepdims=True)

    def taken(value, q):
        return pltpu.roll(value, LANES - 8 * q, 1)

    steps = totals / taken(totals, 1)
    gap = steps - taken(every, 3)
    norms = jnp.sum(taken(every, 4) + gap * (gap * taken(every, 2) - 2.0 * taken(every, 5)), axis=0, keepdims=True)
    ratios = norms / totals
    alpha0 = [steps[:, c:c + 1] for c in range(chans)]
    norm1 = [norms[:, c:c + 1] for c in range(chans)]
    beta = [ratios[:, c:c + 1] for c in range(chans)]

    def combined(ref, side, c, *index):
        own = ref[(0, side, c) + index]
        return (own - alpha0[c] * ref[(1, side, c) + index]) + beta[c] * own

    products = []
    for c in range(chans):
        for f in range(frames):
            residual = bv[c, f] - alpha0[c] * av[c, f]
            rv[c, f] = residual
            pv[c, f] = residual + beta[c] * bv[c, f]
        product = 0.0
        for f in range(frames):
            image = (iv[c, f] - alpha0[c] * qv[c, f]) + beta[c] * iv[c, f]
            qv[c, f] = image
            product = product + pv[c, f] * image
        products.append(product[:half] + product[half:])
    for c in range(chans):
        for copy in wait_early[c]:
            copy.wait_recv()
        upper, lower = slice(0, half), slice(half, rows)
        prior = pv[c, 0, upper] - combined(hz, 0, c, upper)
        after = pv[c, frames - 1, lower] - combined(hz, 1, c, lower)
        products[c] = products[c] + hwt[upper] * prior * prior + wtv[frames - 1, lower] * after * after
    before = list(sends)
    exchange(1, {(0, c): whole_sum(products[c]) for c in range(chans)})
    for c in range(chans):
        for copy in wait_late[c]:
            copy.wait_recv()
        for f in sorted({0, frames - 1}):
            qv[c, f] = qv[c, f] + outer(c, f, pv, combined)
    for copy in before:
        copy.wait_send()
    curvatures = jnp.sum(collect(1), axis=0, keepdims=True)
    for c in range(chans):
        alpha1 = norm1[c] / curvatures[:, c:c + 1]
        for f in range(frames):
            x_out[c, f] = alpha0[c] * bv[c, f] + alpha1 * pv[c, f]
            r_out[c, f] = rv[c, f] - alpha1 * qv[c, f]
    for copy in sends[len(before):]:
        copy.wait_send()


def shards(sizes, right_side, screening, time_weight, row_weight, column_weight):
    tms, bands, strips = sizes
    chans, frames, rows, cols = right_side.shape
    f32 = jnp.float32
    field = pltpu.VMEM((chans, frames, rows, cols), f32)
    coefficient = pltpu.VMEM((frames, rows, cols), f32)
    tall = -(-2 * frames // 8) * 8
    devices = tms * bands * strips
    dma = pltpu.SemaphoreType.DMA
    anywhere = pl.BlockSpec(memory_space=pltpu.HBM)
    inside = pl.BlockSpec(memory_space=pltpu.VMEM)
    return pl.pallas_call(
        functools.partial(kernel, sizes),
        out_shape=(pltpu.VMEM(right_side.shape, f32),) * 2,
        in_specs=[anywhere] * 5,
        out_specs=(inside, inside),
        scratch_shapes=[field] + [coefficient] * 6 + [field] * 5 + [
            pltpu.VMEM((2, 2, chans, rows, cols), f32),
            pltpu.VMEM((rows, cols), f32),
            pltpu.VMEM((2, 2, chans, tall, cols), f32),
            pltpu.VMEM((2, 2, chans, tall, cols), f32),
            pltpu.VMEM((2, 2, chans, frames, rows, LANES), f32),
            pltpu.VMEM((frames, rows, LANES), f32),
            pltpu.VMEM((2, devices, 1, LANES), f32),
            dma((5,)),
            dma((2, 2, chans, 2)), dma((2, 2, chans, 2)), dma, dma,
            dma((2, 2, chans)), dma((2, 2, chans)),
            dma((2, 2, chans)), dma((2, 2, chans)), dma, dma,
            dma((2, devices)), dma((2, devices)),
        ],
        compiler_params=pltpu.CompilerParams(
            collective_id=0, has_side_effects=True, vmem_limit_bytes=VMEM_BYTES),
        cost_estimate=pl.CostEstimate(flops=10_000_000, bytes_accessed=2_000_000, transcendentals=0),
    )(right_side, screening, time_weight, row_weight, column_weight)


def solution(mesh):
    field = P(None, ("clip", "tm"), "row", "col")
    coefficient = P(("clip", "tm"), "row", "col")
    sizes = tuple(mesh.shape[a] for a in ("tm", "row", "col"))
    return jax.shard_map(
        functools.partial(shards, sizes),
        mesh=mesh,
        in_specs=(field,) + (coefficient,) * 4,
        out_specs=(field, field),
        check_vma=False,
    )
```
